256 devices in a mesh: row: 8 (over y, z_hi), col: 4 (over x), tok: 8 (over z_lo, core).
Axes of the slice: x: 4, y: 4, z: 8 (z_hi: 2, z_lo: 4; z = z_hi * 4 + z_lo), core: 2. Of those that a mesh axis runs over, the one named last changes fastest.
Arguments:
- first_inputs: bfloat16 [2048, 8192], P(('row', 'col'), 'tok'), may hold values from -12 to 12, as said below
- second_inputs: bfloat16 [2048, 8192], P(('row', 'col'), 'tok'), may hold values from -12 to 12, as said below
- first_weights: bfloat16 [8192, 2, 14336], P('tok', None, ('row', 'col')), may hold values from -0.0625 to 0.0625
- second_weights: bfloat16 [8192, 2, 14336], P('tok', None, ('col', 'row')), may hold values from -0.0625 to 0.0625
Outputs:
- unit_scores: float32 [14336, 14336], P(('row', 'tok'), 'col')
The draws below stay inside these ranges and needn't reach their ends.
Inputs may be any that keep to these rules, and one draw needn't show every extreme that they name: `first_inputs`: the first model's layer input for each calibration token. `second_inputs`: the second model's layer input for each calibration token.
All inputs are finite; a program needn't handle non-finite values.
Results may differ from the reference program's by a relative error of at most 0.015.
Values may be sent and summed in bfloat16 or wider, within the bound.
No kernel may reach another device: no remote copies, remote signals or barrier semaphores. Data moves between devices by JAX's collectives and lax.ppermute only.
A program may use at most 128 MiB of HBM per device.

```python
import jax
import jax.numpy as jnp
from jax import lax

D = 8192
UNITS_A = 14336
UNITS_B = 14336
TOK_DEV = 256
TOKENS = 2048


def token_rise(lower, upper):
    position = jnp.arange(TOKENS, dtype=jnp.float32)[:, None]
    return lower + (upper - lower) * position / max(TOKENS - 1, 1)


def draw_first_inputs(key, part):
    key = jax.random.fold_in(key, 11)
    key_one = jax.random.fold_in(key, 0)
    key_three = jax.random.fold_in(key, 2)
    common = jax.random.normal(key_three, (1, D), jnp.float32)
    values = jax.random.normal(key_one, (TOKENS, D), jnp.float32) + token_rise(0.4, 1.6) * common
    return jnp.clip(values, -12.0, 12.0).astype(jnp.bfloat16)


def draw_second_inputs(key, part):
    key = jax.random.fold_in(key, 23)
    key_one = jax.random.fold_in(key, 0)
    key_three = jax.random.fold_in(key, 2)
    common = jax.random.normal(key_three, (1, D), jnp.float32)
    values = jax.random.normal(key_one, (TOKENS, D), jnp.float32) + 0.8 * common
    return jnp.clip(values, -12.0, 12.0).astype(jnp.bfloat16)


def steps_of(own_key, dims, shards, low, top_value):
    loudness = 1.0
    for dim, parts in shards:
        steps = jax.random.uniform(jax.random.fold_in(jax.random.fold_in(own_key, 6), dim), (parts,), jnp.float32, low / len(shards), top_value / len(shards))
        loudness = loudness * jnp.repeat(jnp.exp(steps), dims[dim] // parts).reshape((-1,) + (1,) * (len(dims) - 1 - dim))
    return loudness


def bell_draw(own_key, shape, scale, bound, cuts=(), held_as=jnp.bfloat16):
    entries = scale * jax.random.normal(own_key, shape, jnp.float32)
    if cuts:
        entries = entries * steps_of(own_key, shape, cuts, -0.22, 0.18)
    return jnp.clip(entries, -bound, bound).astype(held_as)


def setup_inputs(seed: int = 0) -> dict:
    streams_of = jax.random.split(jax.random.key(seed), 5)
    first_inputs = draw_first_inputs(jax.random.fold_in(streams_of[4], 71), 0)
    second_inputs = draw_second_inputs(jax.random.fold_in(streams_of[4], 71), 0)
    first_weights = bell_draw(streams_of[2], (D, 2, UNITS_A), D ** -0.5, 0.0625, ((0, 8), (2, 32)))
    second_weights = bell_draw(streams_of[3], (D, 2, UNITS_B), D ** -0.5, 0.0625, ((0, 8), (2, 32)))
    return dict(first_inputs=first_inputs, second_inputs=second_inputs, first_weights=first_weights, second_weights=second_weights)


def normalized(inputs, weights):
    gate = jnp.dot(inputs, weights[:, 0, :], preferred_element_type=jnp.float32)
    upward = jnp.dot(inputs, weights[:, 1, :], preferred_element_type=jnp.float32)
    activity = jax.nn.silu(gate) * upward
    center = lax.optimization_barrier(jnp.mean(activity, axis=0))
    deviation = activity - center
    spread = lax.optimization_barrier(jnp.mean(deviation * deviation, axis=0))
    return (deviation * lax.rsqrt(spread + 1e-05)).astype(jnp.bfloat16)

def reference(first_inputs, second_inputs, first_weights, second_weights):
    norm_first = normalized(first_inputs, first_weights)
    norm_second = normalized(second_inputs, second_weights)
    total = jnp.zeros((UNITS_A, UNITS_B), jnp.float32)
    for block in range(TOKENS // TOK_DEV):
        rows_first = norm_first[block * TOK_DEV:(block + 1) * TOK_DEV]
        rows_second = norm_second[block * TOK_DEV:(block + 1) * TOK_DEV]
        partial_term = jnp.dot(rows_first.T, rows_second, preferred_element_type=jnp.float32)
        rounded = lax.optimization_barrier(partial_term.astype(jnp.bfloat16))
        total = total + rounded.astype(jnp.float32)
    return total * float(TOKENS) ** (-0.5)
```

```python
import itertools

import jax
import jax.numpy as jnp
from jax import lax
from jax.sharding import Mesh, PartitionSpec as P

AXES = ("y", "zh", "x", "a", "b", "c")
SIZES = dict(y=4, zh=2, x=4, a=2, b=2, c=2)


def move(value, axes, target):
    sizes = [SIZES[axis] for axis in axes]
    pairs = []
    for source, place in enumerate(itertools.product(*[range(size) for size in sizes])):
        goal = target(**dict(zip(axes, place)))
        index = 0
        for size, coordinate in zip(sizes, goal):
            index = index * size + coordinate % size
        pairs.append((source, index))
    return lax.ppermute(value, axes, pairs)


def shift(value, axis, step):
    return move(value, (axis,), lambda **place: (place[axis] + step,))


def swap(value, axis):
    return shift(value, axis, 1)


def ring(value, axis, cut):
    before = shift(value, axis, 1)
    after = shift(value, axis, -1)
    half = value.shape[cut] // 2
    far_low = shift(lax.slice_in_dim(before, 0, half, axis=cut), axis, 1)
    far_high = shift(lax.slice_in_dim(after, half, 2 * half, axis=cut), axis, -1)
    return value, before, after, jnp.concatenate([far_low, far_high], axis=cut)


def placed(blocks, axis, dim):
    me = lax.axis_index(axis)
    shape = list(blocks[0].shape)
    shape.insert(dim, 4)
    whole = jnp.zeros(shape, blocks[0].dtype)
    for block, step in zip(blocks, (0, 3, 1, 2)):
        whole = lax.dynamic_update_index_in_dim(whole, block, (me + step) % 4, dim)
    return whole


def gather_plane(first, second, cut):
    first = placed(ring(first, "x", cut), "x", 0)
    second = placed(ring(second, "y", cut), "y", 0)
    first = placed(ring(first, "y", cut + 1), "y", 0)
    second = placed(ring(second, "x", cut + 1), "x", 1)
    return first, second


def local(first_inputs, second_inputs, first_weights, second_weights):
    a, b, c, zh = (lax.axis_index(name) for name in ("a", "b", "c", "zh"))
    depth, _, units = first_weights.shape
    tokens = first_inputs.shape[0] * 32
    quarter = units // 4
    is_first = b == 0
    weights = first_weights.reshape(depth, 2 * units), second_weights.reshape(depth, 2 * units)
    sent_weights = jnp.where(is_first, weights[1], weights[0])
    own_weights = jnp.where(is_first, weights[0], weights[1])
    sent_inputs = jnp.where(is_first, second_inputs, first_inputs)
    own_inputs = jnp.where(is_first, first_inputs, second_inputs)
    came_inputs = swap(sent_inputs, "b")
    came_weights = swap(sent_weights, "b")

    piece = jnp.concatenate([own_inputs, came_inputs], axis=1)
    other = swap(piece, "zh")
    low, high = jnp.where(zh == 0, piece, other), jnp.where(zh == 0, other, piece)
    low, high = gather_plane(low, high, 1)
    full = jnp.concatenate([low.reshape(-1, 2 * depth), high.reshape(-1, 2 * depth)], axis=0)

    def term(matrix, part):
        return lax.dot_general(
            matrix,
            lax.slice_in_dim(full, part * depth, (part + 1) * depth, axis=1),
            (((0,), (1,)), ((), ())),
            preferred_element_type=jnp.float32,
        )

    partial_sums = (term(own_weights, 0) + term(came_weights, 1)).reshape(2, 2, 2 * quarter, tokens)
    sent = lax.dynamic_index_in_dim(partial_sums, 1 - c, 1, keepdims=False).astype(jnp.bfloat16)
    kept = lax.dynamic_index_in_dim(partial_sums, c, 1, keepdims=False)
    sums = (kept + swap(sent, "c").astype(jnp.float32)).reshape(2, 2, quarter, tokens)
    sent = lax.dynamic_index_in_dim(sums, 1 - a, 1, keepdims=False).astype(jnp.bfloat16)
    kept = lax.dynamic_index_in_dim(sums, a, 1, keepdims=False)
    gate_up = kept + swap(sent, "a").astype(jnp.float32)

    act = jax.nn.silu(gate_up[0]) * gate_up[1]
    deviation = act - jnp.mean(act, axis=1, keepdims=True)
    spread = jnp.mean(deviation * deviation, axis=1, keepdims=True)
    norm = (deviation * lax.rsqrt(spread + 1e-05)).astype(jnp.bfloat16)

    eighth = quarter // 2
    came = swap(jnp.where(is_first, norm[eighth:], norm[:eighth]), "b")
    one = jnp.where(is_first, norm[:eighth], came)
    two = jnp.where(is_first, came, norm[eighth:])
    one = move(one, ("x", "a", "b"), lambda x, a, b: (2 * a + b, x // 2, x % 2))
    one_low, one_high = gather_plane(one[:, : tokens // 2], one[:, tokens // 2 :], 1)
    two = lax.all_gather(two, ("zh", "a", "b"), axis=0, tiled=True)
    two_core = swap(two, "c")
    pair = jnp.stack([jnp.where(c == 0, two, two_core), jnp.where(c == 0, two_core, two)])
    pair = pair.reshape(2, 2, 2 * quarter, tokens).transpose(1, 0, 2, 3).reshape(8 * quarter, tokens)

    def score(left, right):
        return lax.dot_general(
            left.reshape(8 * quarter, tokens // 2),
            right,
            (((1,), (1,)), ((), ())),
            preferred_element_type=jnp.float32,
        )

    scores = score(one_low, pair[:, : tokens // 2]) + score(one_high, pair[:, tokens // 2 :])
    scores = (scores * float(tokens) ** (-0.5)).astype(jnp.bfloat16).reshape(4, 2 * quarter, 8 * quarter)
    scores = lax.all_to_all(scores, "y", 0, 0, tiled=True)
    return jnp.concatenate([scores[i] for i in range(4)], axis=1).astype(jnp.float32)


def solution(mesh):
    fine = Mesh(mesh.devices.reshape([SIZES[axis] for axis in AXES]), AXES)
    specs = (
        P(("y", "zh", "x"), ("a", "b", "c")),
        P(("y", "zh", "x"), ("a", "b", "c")),
        P(("a", "b", "c"), None, ("y", "zh", "x")),
        P(("a", "b", "c"), None, ("x", "y", "zh")),
    )
    return jax.shard_map(
        local, mesh=fine, in_specs=specs, out_specs=P(("y", "zh", "a", "b", "c"), "x"), check_vma=False
    )
```

```python
import functools
import itertools

import jax
import jax.numpy as jnp
from jax import lax
from jax.experimental import pallas as pl
from jax.experimental.pallas import tpu as pltpu
from jax.sharding import Mesh, PartitionSpec as P

AXES = ("y", "zh", "x", "a", "b", "c")
SIZES = dict(y=4, zh=2, x=4, a=2, b=2, c=2)


def move(value, axes, target):
    sizes = [SIZES[axis] for axis in axes]
    pairs = []
    for source, place in enumerate(itertools.product(*[range(size) for size in sizes])):
        goal = target(**dict(zip(axes, place)))
        if goal is None:
            continue
        index = 0
        for size, coordinate in zip(sizes, goal):
            index = index * size + coordinate % size
        pairs.append((source, index))
    return lax.ppermute(value, axes, pairs)


def swap(value, axis):
    return move(value, (axis,), lambda **place: (place[axis] + 1,))


MASKS = (0, 1, 3, 2)


def plane(value, stage, mask):
    return move(
        value, ("y", "x", "c"), lambda y, x, c: (y, x ^ mask, c) if c == stage else (y ^ mask, x, c)
    )


def direct(value):
    return value, plane(value, 0, 1), plane(value, 0, 3), plane(value, 0, 2)


def ring(value, cut, *first):
    one = plane(value, 1, 1)
    three = plane(value, 1, 3)
    if first:
        one, three, *first = lax.optimization_barrier((one, three, *first))
    half = value.shape[cut] // 2
    far_low = plane(lax.slice_in_dim(one, 0, half, axis=cut), 1, 3)
    far_high = plane(lax.slice_in_dim(three, half, 2 * half, axis=cut), 1, 1)
    return value, one, three, far_low, far_high, *first


def absolute(value, me, dim):
    shape = value.shape
    value = value.reshape(*shape[:dim], 2, 2, *shape[dim + 1 :])
    low, high = (lax.index_in_dim(value, i, dim) for i in range(2))
    value = jnp.concatenate([low, lax.rev(high, (dim + 1,))], axis=dim)
    value = jnp.where(me % 2 == 0, value, lax.rev(value, (dim + 1,)))
    value = jnp.where(me // 2 == 0, value, lax.rev(value, (dim,)))
    return value.reshape(shape)


def product_kernel(ranges, tiles, count, *refs):
    weights, inputs = refs[:count], refs[count : count + len(ranges)]
    kept_ref, sent_ref, held_weights, held, arrived = refs[count + len(ranges) :]
    width = inputs[0].shape[1]
    pieces, column, row = [], 0, 0
    for ref in weights:
        pieces.append((ref, held_weights.at[:, pl.ds(column, ref.shape[1])]))
        column += ref.shape[1]
    for ref, (start, blocks) in zip(inputs, ranges):
        pieces.append((ref.at[pl.ds(start, blocks)], held.at[pl.ds(row, blocks)]))
        row += blocks
    copies = [pltpu.make_async_copy(*piece, arrived.at[i]) for i, piece in enumerate(pieces)]
    for copy in copies:
        copy.start()
    for copy in copies[:count]:
        copy.wait()
    done, waited = 0, count
    for blocks, needed in tiles:
        for copy in copies[waited : count + needed]:
            copy.wait()
        waited = count + needed
        sums = lax.dot_general(
            held_weights[...],
            held[done : done + blocks].reshape(blocks * width, column),
            (((1,), (1,)), ((), ())),
            preferred_element_type=jnp.float32,
        )
        for i in range(blocks):
            block = sums[:, i * width : (i + 1) * width].reshape(2, *kept_ref.shape[1:])
            kept_ref[done + i] = block[0]
            sent_ref[done + i] = block[1].astype(sent_ref.dtype)
        done += blocks


def called(kernel, out_shape, scratch_shapes, *arrays, scalars=(), space=pltpu.VMEM):
    vmem = pl.BlockSpec(memory_space=pltpu.VMEM)
    return pl.pallas_call(
        kernel,
        out_shape=out_shape,
        in_specs=[pl.BlockSpec(memory_space=pltpu.SMEM)] * len(scalars)
        + [pl.BlockSpec(memory_space=space)] * len(arrays),
        out_specs=jax.tree.map(lambda _: vmem, out_shape),
        scratch_shapes=scratch_shapes,
        compiler_params=pltpu.CompilerParams(vmem_limit_bytes=48 * 1024 * 1024),
        cost_estimate=pl.CostEstimate(flops=1, bytes_accessed=1, transcendentals=0),
    )(*scalars, *arrays)


def products(weights, inputs, ranges, tiles):
    units, count = weights[0].shape[0], sum(blocks for _, blocks in ranges)
    _, width, depth = inputs[0].shape
    shape = (count, 2, units // 4, width)
    return called(
        functools.partial(product_kernel, ranges, tiles, len(weights)),
        (jax.ShapeDtypeStruct(shape, jnp.float32), jax.ShapeDtypeStruct(shape, jnp.bfloat16)),
        [
            pltpu.VMEM((units, depth), weights[0].dtype),
            pltpu.VMEM((count, width, depth), weights[0].dtype),
            pltpu.SemaphoreType.DMA((len(weights) + len(inputs),)),
        ],
        *weights,
        *inputs,
        space=pl.ANY,
    )


def norm_kernel(position_ref, *refs):
    sums, (out_ref, act) = refs[:-2], refs[-2:]
    total = 0.0
    count, _, width = act.shape
    done = 0
    for kept_ref, came_ref in zip(sums[::2], sums[1::2]):
        for i in range(kept_ref.shape[0]):
            gate = kept_ref[i, 0] + came_ref[i, 0].astype(jnp.float32)
            up = kept_ref[i, 1] + came_ref[i, 1].astype(jnp.float32)
            value = gate / (1.0 + jnp.exp(-gate)) * up
            act[done] = value
            total += value
            done += 1
    inverse = 1.0 / (count * width)
    mean = jnp.sum(total, axis=1, keepdims=True) * inverse
    squares = 0.0
    for i in range(count):
        deviation = act[i] - mean
        squares += deviation * deviation
    scale = lax.rsqrt(jnp.sum(squares, axis=1, keepdims=True) * inverse + 1e-05)
    for i in range(count):
        place = pl.multiple_of(position_ref[i] * width, width)
        out_ref[:, pl.ds(place, width)] = ((act[i] - mean) * scale).astype(out_ref.dtype)


def normalized(positions, *sums):
    count = positions.shape[0]
    _, _, units, width = sums[0].shape
    return called(
        norm_kernel,
        jax.ShapeDtypeStruct((units, count * width), jnp.bfloat16),
        [pltpu.VMEM((count, units, width), jnp.float32)],
        *sums,
        scalars=(positions,),
    )


def local(first_inputs, second_inputs, first_weights, second_weights):
    a, b, c, x, y, zh = (lax.axis_index(name) for name in ("a", "b", "c", "x", "y", "zh"))
    depth, _, units = first_weights.shape
    piece = first_inputs.shape[0]
    tokens = piece * 32
    half, quarter, eighth = units // 2, units // 4, units // 8
    is_first = b == 0
    sent_inputs = jnp.where(is_first, second_inputs, first_inputs)
    own_inputs = jnp.where(is_first, first_inputs, second_inputs)
    own_zh = jnp.concatenate([own_inputs, swap(sent_inputs, "b")], axis=1)
    other_zh = jnp.concatenate(
        [swap(own_inputs, "zh"), move(sent_inputs, ("zh", "b"), lambda zh, b: (zh + 1, b + 1))], axis=1
    )

    def turned_weights(model):
        parts = model.transpose(1, 2, 0).reshape(2, 2, half, depth).swapaxes(0, 1)
        return jnp.where(c == 0, parts, lax.rev(parts, (0,))).reshape(2 * units, depth)

    sent_weights = turned_weights(jnp.where(is_first, second_weights, first_weights))
    own_weights = turned_weights(jnp.where(is_first, first_weights, second_weights))
    split = depth * 3 // 8
    came_one, came_two = swap(sent_weights[:, :split], "b"), swap(sent_weights[:, split:], "b")

    block = jnp.concatenate(
        [jnp.where(zh == 0, own_zh, other_zh), jnp.where(zh == 0, other_zh, own_zh)], axis=0
    )
    block, came_one = lax.optimization_barrier((jnp.stack(direct(block)), came_one))
    own, one, three, far_low, far_high, came_two = ring(block, 0, came_two)
    weights = own_weights, came_one, came_two

    def core_sum(kept, sent, order):
        came = swap(sent, "c")
        came = jnp.stack([came[i] for i in order])
        return (kept + came.astype(jnp.float32)).reshape(-1, 2, 2, quarter, 2 * piece)

    def depth_parts(sums):
        sent = lax.dynamic_index_in_dim(sums, 1 - a, 2, keepdims=False).astype(jnp.bfloat16)
        kept = lax.dynamic_index_in_dim(sums, a, 2, keepdims=False)
        return [kept[:, :, :eighth], kept[:, :, eighth:]], [sent[:, :, :eighth], sent[:, :, eighth:]]

    early_blocks = [(i, j) for i in range(3) for j in range(3)]
    late_blocks = [(i, 3) for i in range(3)] + [(3, j) for j in range(4)]
    turned = [[blocks.index((j, i)) for i, j in blocks] for blocks in (early_blocks, late_blocks)]
    early = products(weights, (own, one, three), ((0, 3),) * 3, ((2, 1), (4, 2), (3, 3)))
    early, far_low, far_high = lax.optimization_barrier((early, far_low, far_high))
    early = core_sum(*early, turned[0])
    early, far_low, far_high = lax.optimization_barrier((early, far_low, far_high))
    early, early_came = depth_parts(early)
    early_came = [swap(part, "a") for part in early_came]
    late = products(
        weights,
        (own, one, three, far_low, far_high),
        ((3, 1),) * 3 + ((0, 2),) * 2,
        ((4, 4), (3, 5)),
    )
    late, early_came[0] = lax.optimization_barrier((late, early_came[0]))
    late = core_sum(*late, turned[1])
    late, early_came[1] = lax.optimization_barrier((late, early_came[1]))
    late, late_came = depth_parts(late)
    late_came = [swap(part, "a") for part in late_came]

    first, second = jnp.where(c == 0, x, y), jnp.where(c == 0, y, x)
    positions = []
    for i, j in early_blocks + late_blocks:
        mine, yours = second ^ MASKS[i], first ^ MASKS[j]
        positions.append(jnp.where(c == 0, mine * 4 + yours, yours * 4 + mine))
    positions = jnp.stack(positions)
    norm = [normalized(positions, early[h], early_came[h], late[h], late_came[h]) for h in range(2)]

    two = move(norm[0], ("b",), lambda b: (0,) if b == 1 else None)
    came = [
        move(norm[h], ("x", "a", "b"), lambda x, a, b: (2 * a + h, x // 2, x % 2) if b == 0 else None)
        for h in range(2)
    ]
    one = jnp.where(x % 2 == 0, came[0], came[1])
    two = jnp.where(is_first, two, norm[1])
    two = lax.all_gather(two, ("zh", "a", "b"), axis=0, tiled=True)
    *one, two = ring(jnp.stack(direct(one)), 2, two)
    two_core = swap(two, "c")
    pair = jnp.stack([jnp.where(c == 0, two, two_core), jnp.where(c == 0, two_core, two)])
    pair = pair.reshape(2, 2, half, tokens).transpose(1, 0, 2, 3).reshape(4 * half, tokens)

    *one, pair = lax.optimization_barrier((*one, pair))
    one = jnp.stack([*one[:3], jnp.concatenate(one[3:], axis=2)])

    scores = lax.dot_general(
        one.reshape(4 * half, tokens), pair, (((1,), (1,)), ((), ())), preferred_element_type=jnp.float32
    )
    scores = (scores * float(tokens) ** (-0.5)).astype(jnp.bfloat16).reshape(4, 4, eighth, 4 * half)
    scores = jnp.where(c == 0, scores, scores.swapaxes(0, 1))
    scores = absolute(absolute(scores, y, 0), x, 1).reshape(4, half, 4 * half)
    scores = lax.all_to_all(scores, "y", 0, 0, tiled=True)
    return jnp.concatenate([scores[i] for i in range(4)], axis=1).astype(jnp.float32)


def solution(mesh):
    fine = Mesh(mesh.devices.reshape([SIZES[axis] for axis in AXES]), AXES)
    specs = (
        P(("y", "zh", "x"), ("a", "b", "c")),
        P(("y", "zh", "x"), ("a", "b", "c")),
        P(("a", "b", "c"), None, ("y", "zh", "x")),
        P(("a", "b", "c"), None, ("x", "y", "zh")),
    )
    return jax.shard_map(
        local, mesh=fine, in_specs=specs, out_specs=P(("y", "zh", "a", "b", "c"), "x"), check_vma=False
    )
```

```python
import functools
import itertools

import jax
import jax.numpy as jnp
from jax import lax
from jax.experimental import pallas as pl
from jax.experimental.pallas import tpu as pltpu
from jax.sharding import Mesh, PartitionSpec as P

AXES = ("y", "zh", "x", "a", "b", "c")
SIZES = dict(y=4, zh=2, x=4, a=2, b=2, c=2)


def move(value, axes, target):
    sizes = [SIZES[axis] for axis in axes]
    pairs = []
    for source, place in enumerate(itertools.product(*[range(size) for size in sizes])):
        goal = target(**dict(zip(axes, place)))
        if goal is None:
            continue
        index = 0
        for size, coordinate in zip(sizes, goal):
            index = index * size + coordinate % size
        pairs.append((source, index))
    return lax.ppermute(value, axes, pairs)


def swap(value, axis):
    return move(value, (axis,), lambda **place: (place[axis] + 1,))


MASKS = (0, 1, 3, 2)


def plane(value, stage, mask):
    return move(
        value, ("y", "x", "c"), lambda y, x, c: (y, x ^ mask, c) if c == stage else (y ^ mask, x, c)
    )


def direct(value):
    return value, plane(value, 0, 1), plane(value, 0, 3), plane(value, 0, 2)


def ring(value, cut, *first):
    one = plane(value, 1, 1)
    three = plane(value, 1, 3)
    if first:
        one, three, *first = lax.optimization_barrier((one, three, *first))
    half = value.shape[cut] // 2
    far_low = plane(lax.slice_in_dim(one, 0, half, axis=cut), 1, 3)
    far_high = plane(lax.slice_in_dim(three, half, 2 * half, axis=cut), 1, 1)
    return value, one, three, far_low, far_high, *first


def absolute(value, me, dim):
    shape = value.shape
    value = value.reshape(*shape[:dim], 2, 2, *shape[dim + 1 :])
    low, high = (lax.index_in_dim(value, i, dim) for i in range(2))
    value = jnp.concatenate([low, lax.rev(high, (dim + 1,))], axis=dim)
    value = jnp.where(me % 2 == 0, value, lax.rev(value, (dim + 1,)))
    value = jnp.where(me // 2 == 0, value, lax.rev(value, (dim,)))
    return value.reshape(shape)


def product_kernel(ranges, tiles, turned, count, *refs):
    weights, inputs = refs[:count], refs[count : count + len(ranges)]
    kept_ref, sent_ref, held_weights, held, arrived = refs[count + len(ranges) :]
    width = inputs[0].shape[1]
    pieces, column, row = [], 0, 0
    for ref in weights:
        pieces.append((ref, held_weights.at[:, pl.ds(column, ref.shape[1])]))
        column += ref.shape[1]
    for ref, (start, blocks) in zip(inputs, ranges):
        pieces.append((ref.at[pl.ds(start, blocks)], held.at[pl.ds(row, blocks)]))
        row += blocks
    copies = [pltpu.make_async_copy(*piece, arrived.at[i]) for i, piece in enumerate(pieces)]
    for copy in copies:
        copy.start()
    for copy in copies[:count]:
        copy.wait()
    done, waited = 0, count
    for blocks, needed in tiles:
        for copy in copies[waited : count + needed]:
            copy.wait()
        waited = count + needed
        sums = lax.dot_general(
            held_weights[...],
            held[done : done + blocks].reshape(blocks * width, column),
            (((1,), (1,)), ((), ())),
            preferred_element_type=jnp.float32,
        )
        for i in range(blocks):
            block = sums[:, i * width : (i + 1) * width].reshape(2, *kept_ref.shape[1:])
            kept_ref[done + i] = block[0]
            sent_ref[turned[done + i]] = block[1].astype(sent_ref.dtype)
        done += blocks


def called(kernel, out_shape, scratch_shapes, *arrays, scalars=(), space=pltpu.VMEM):
    vmem = pl.BlockSpec(memory_space=pltpu.VMEM)
    return pl.pallas_call(
        kernel,
        out_shape=out_shape,
        in_specs=[pl.BlockSpec(memory_space=pltpu.SMEM)] * len(scalars)
        + [pl.BlockSpec(memory_space=space)] * len(arrays),
        out_specs=jax.tree.map(lambda _: vmem, out_shape),
        scratch_shapes=scratch_shapes,
        compiler_params=pltpu.CompilerParams(vmem_limit_bytes=48 * 1024 * 1024),
        cost_estimate=pl.CostEstimate(flops=1, bytes_accessed=1, transcendentals=0),
    )(*scalars, *arrays)


def products(weights, inputs, ranges, tiles, blocks):
    turned = [blocks.index(place[::-1]) for place in blocks]
    units, count = weights[0].shape[0], len(blocks)
    _, width, depth = inputs[0].shape
    shape = (count, 2, units // 4, width)
    return called(
        functools.partial(product_kernel, ranges, tiles, turned, len(weights)),
        (jax.ShapeDtypeStruct(shape, jnp.float32), jax.ShapeDtypeStruct(shape, jnp.bfloat16)),
        [
            pltpu.VMEM((units, depth), weights[0].dtype),
            pltpu.VMEM((count, width, depth), weights[0].dtype),
            pltpu.SemaphoreType.DMA((len(weights) + len(inputs),)),
        ],
        *weights,
        *inputs,
        space=pl.ANY,
    )


def norm_kernel(position_ref, *refs):
    sums, (out_ref, act) = refs[:-2], refs[-2:]
    total = 0.0
    count, _, width = act.shape
    done = 0
    for kept_ref, came_ref in zip(sums[::2], sums[1::2]):
        for i in range(kept_ref.shape[0]):
            gate = kept_ref[i, 0] + came_ref[i, 0].astype(jnp.float32)
            up = kept_ref[i, 1] + came_ref[i, 1].astype(jnp.float32)
            value = gate / (1.0 + jnp.exp(-gate)) * up
            act[done] = value
            total += value
            done += 1
    inverse = 1.0 / (count * width)
    mean = jnp.sum(total, axis=1, keepdims=True) * inverse
    squares = 0.0
    for i in range(count):
        deviation = act[i] - mean
        squares += deviation * deviation
    scale = lax.rsqrt(jnp.sum(squares, axis=1, keepdims=True) * inverse + 1e-05)
    for i in range(count):
        place = pl.multiple_of(position_ref[i] * width, width)
        out_ref[:, pl.ds(place, width)] = ((act[i] - mean) * scale).astype(out_ref.dtype)


def normalized(positions, *sums):
    count = positions.shape[0]
    _, _, units, width = sums[0].shape
    return called(
        norm_kernel,
        jax.ShapeDtypeStruct((units, count * width), jnp.bfloat16),
        [pltpu.VMEM((count, units, width), jnp.float32)],
        *sums,
        scalars=(positions,),
    )


def local(first_inputs, second_inputs, first_weights, second_weights):
    a, b, c, x, y, zh = (lax.axis_index(name) for name in ("a", "b", "c", "x", "y", "zh"))
    depth, _, units = first_weights.shape
    piece = first_inputs.shape[0]
    tokens = piece * 32
    half, quarter, eighth = units // 2, units // 4, units // 8
    is_first = b == 0
    sent_inputs = jnp.where(is_first, second_inputs, first_inputs)
    own_inputs = jnp.where(is_first, first_inputs, second_inputs)
    own_zh = jnp.concatenate([own_inputs, swap(sent_inputs, "b")], axis=1)
    other_zh = jnp.concatenate(
        [swap(own_inputs, "zh"), move(sent_inputs, ("zh", "b"), lambda zh, b: (zh + 1, b + 1))], axis=1
    )

    def turned_weights(model):
        parts = model.transpose(1, 2, 0).reshape(2, 2, half, depth).swapaxes(0, 1)
        return jnp.where(c == 0, parts, lax.rev(parts, (0,))).reshape(2 * units, depth)

    sent_weights = turned_weights(jnp.where(is_first, second_weights, first_weights))
    own_weights = turned_weights(jnp.where(is_first, first_weights, second_weights))
    split = depth * 3 // 8
    came_one, came_two = swap(sent_weights[:, :split], "b"), swap(sent_weights[:, split:], "b")

    block = jnp.concatenate(
        [jnp.where(zh == 0, own_zh, other_zh), jnp.where(zh == 0, other_zh, own_zh)], axis=0
    )
    block, came_one = lax.optimization_barrier((jnp.stack(direct(block)), came_one))
    own, one, three, far_low, far_high, came_two = ring(block, 0, came_two)
    weights = own_weights, came_one, came_two

    def core_sum(kept, came):
        return (kept + came.astype(jnp.float32)).reshape(-1, 2, 2, quarter, 2 * piece)

    def depth_parts(sums):
        sent = lax.dynamic_index_in_dim(sums, 1 - a, 2, keepdims=False).astype(jnp.bfloat16)
        kept = lax.dynamic_index_in_dim(sums, a, 2, keepdims=False)
        return [kept[:, :, :eighth], kept[:, :, eighth:]], [sent[:, :, :eighth], sent[:, :, eighth:]]

    chunks = (
        [(i, j) for i in range(2) for j in range(2)],
        [(0, 2), (1, 2), (2, 0), (2, 1), (2, 2)],
        [(i, 3) for i in range(3)] + [(3, j) for j in range(4)],
    )
    kept, sent = products(weights, (own, one), ((0, 2), (0, 2)), ((2, 1), (2, 2)), chunks[0])
    came = swap(sent, "c")
    early = products(weights, (own, one, three), ((2, 1), (2, 1), (0, 3)), ((2, 2), (3, 3)), chunks[1])
    early, came, far_low, far_high = lax.optimization_barrier((early, came, far_low, far_high))
    first, first_came = depth_parts(core_sum(kept, came))
    first_came = [swap(part, "a") for part in first_came]
    came = swap(early[1], "c")
    late = products(
        weights,
        (own, one, three, far_low, far_high),
        ((3, 1),) * 3 + ((0, 2),) * 2,
        ((4, 4), (3, 5)),
        chunks[2],
    )
    late, came, first_came = lax.optimization_barrier((late, came, first_came))
    early, early_came = depth_parts(core_sum(early[0], came))
    early_came = [swap(part, "a") for part in early_came]
    late = core_sum(late[0], swap(late[1], "c"))
    late, early_came = lax.optimization_barrier((late, early_came))
    late, late_came = depth_parts(late)
    late_came = [swap(part, "a") for part in late_came]

    inner, outer = jnp.where(c == 0, x, y), jnp.where(c == 0, y, x)
    positions = []
    for i, j in chunks[0] + chunks[1] + chunks[2]:
        mine, yours = outer ^ MASKS[i], inner ^ MASKS[j]
        positions.append(jnp.where(c == 0, mine * 4 + yours, yours * 4 + mine))
    positions = jnp.stack(positions)
    norm = [normalized(positions, first[h], first_came[h], early[h], early_came[h], late[h], late_came[h]) for h in range(2)]

    two = move(norm[0], ("b",), lambda b: (0,) if b == 1 else None)
    came = [
        move(norm[h], ("x", "a", "b"), lambda x, a, b: (2 * a + h, x // 2, x % 2) if b == 0 else None)
        for h in range(2)
    ]
    one = jnp.where(x % 2 == 0, came[0], came[1])
    two, one = lax.optimization_barrier((jnp.where(is_first, two, norm[1]), one))
    two = lax.all_gather(two, ("zh", "a", "b"), axis=0, tiled=True)
    one = ring(jnp.stack(direct(one)), 2)
    one = jnp.stack([*one[:3], jnp.concatenate(one[3:], axis=2)]).reshape(4 * half, tokens)
    two, one = lax.optimization_barrier((two, one))

    def score(columns):
        result = lax.dot_general(one, columns, (((1,), (1,)), ((), ())), preferred_element_type=jnp.float32)
        return (result * float(tokens) ** (-0.5)).astype(jnp.bfloat16)

    other = swap(two, "c")
    mine, other = lax.optimization_barrier((score(two), other))
    other = score(other)
    low, high = jnp.where(c == 0, mine, other), jnp.where(c == 0, other, mine)
    scores = jnp.concatenate([low[:, :half], high[:, :half], low[:, half:], high[:, half:]], axis=1)
    scores = scores.reshape(4, 4, eighth, 4 * half)
    scores = jnp.where(c == 0, scores, scores.swapaxes(0, 1))
    scores = absolute(absolute(scores, y, 0), x, 1).reshape(4, half, 4 * half)
    scores = lax.all_to_all(scores, "y", 0, 0, tiled=True)
    return jnp.concatenate([scores[i] for i in range(4)], axis=1).astype(jnp.float32)


def solution(mesh):
    fine = Mesh(mesh.devices.reshape([SIZES[axis] for axis in AXES]), AXES)
    specs = (
        P(("y", "zh", "x"), ("a", "b", "c")),
        P(("y", "zh", "x"), ("a", "b", "c")),
        P(("a", "b", "c"), None, ("y", "zh", "x")),
        P(("a", "b", "c"), None, ("x", "y", "zh")),
    )
    return jax.shard_map(
        local, mesh=fine, in_specs=specs, out_specs=P(("y", "zh", "a", "b", "c"), "x"), check_vma=False
    )
```

```python
import functools
import itertools

import jax
import jax.numpy as jnp
from jax import lax
from jax.experimental import pallas as pl
from jax.experimental.pallas import tpu as pltpu
from jax.sharding import Mesh, PartitionSpec as P

AXES = ("y", "zh", "x", "a", "b", "c")
SIZES = dict(y=4, zh=2, x=4, a=2, b=2, c=2)


def move(value, axes, target):
    sizes = [SIZES[axis] for axis in axes]
    pairs = []
    for source, place in enumerate(itertools.product(*[range(size) for size in sizes])):
        goal = target(**dict(zip(axes, place)))
        if goal is None:
            continue
        index = 0
        for size, coordinate in zip(sizes, goal):
            index = index * size + coordinate % size
        pairs.append((source, index))
    return lax.ppermute(value, axes, pairs)


def swap(value, axis):
    return move(value, (axis,), lambda **place: (place[axis] + 1,))


MASKS = (0, 1, 3, 2)


def plane(value, stage, mask):
    return move(
        value, ("y", "x", "c"), lambda y, x, c: (y, x ^ mask, c) if c == stage else (y ^ mask, x, c)
    )


def direct(value):
    return value, plane(value, 0, 1), plane(value, 0, 3), plane(value, 0, 2)


def ring(value, cut, *first):
    one = plane(value, 1, 1)
    three = plane(value, 1, 3)
    if first:
        one, three, *first = lax.optimization_barrier((one, three, *first))
    half = value.shape[cut] // 2
    far_low = plane(lax.slice_in_dim(one, 0, half, axis=cut), 1, 3)
    far_high = plane(lax.slice_in_dim(three, half, 2 * half, axis=cut), 1, 1)
    return value, one, three, far_low, far_high, *first


def absolute(value, me, dim):
    shape = value.shape
    value = value.reshape(*shape[:dim], 2, 2, *shape[dim + 1 :])
    low, high = (lax.index_in_dim(value, i, dim) for i in range(2))
    value = jnp.concatenate([low, lax.rev(high, (dim + 1,))], axis=dim)
    value = jnp.where(me % 2 == 0, value, lax.rev(value, (dim + 1,)))
    value = jnp.where(me // 2 == 0, value, lax.rev(value, (dim,)))
    return value.reshape(shape)


def product_kernel(ranges, tiles, turned, count, *refs):
    weights, inputs = refs[:count], refs[count : count + len(ranges)]
    kept_ref, sent_ref, held_weights, held, arrived = refs[count + len(ranges) :]
    width = inputs[0].shape[1]
    pieces, column, row = [], 0, 0
    for ref in weights:
        pieces.append((ref, held_weights.at[:, pl.ds(column, ref.shape[1])]))
        column += ref.shape[1]
    for ref, (start, blocks) in zip(inputs, ranges):
        pieces.append((ref.at[pl.ds(start, blocks)], held.at[pl.ds(row, blocks)]))
        row += blocks
    copies = [pltpu.make_async_copy(*piece, arrived.at[i]) for i, piece in enumerate(pieces)]
    for copy in copies:
        copy.start()
    for copy in copies[:count]:
        copy.wait()
    done, waited = 0, count
    for blocks, needed in tiles:
        for copy in copies[waited : count + needed]:
            copy.wait()
        waited = count + needed
        sums = lax.dot_general(
            held_weights[...],
            held[done : done + blocks].reshape(blocks * width, column),
            (((1,), (1,)), ((), ())),
            preferred_element_type=jnp.float32,
        )
        for i in range(blocks):
            block = sums[:, i * width : (i + 1) * width].reshape(2, *kept_ref.shape[1:])
            kept_ref[done + i] = block[0]
            sent_ref[turned[done + i]] = block[1].astype(sent_ref.dtype)
        done += blocks


def called(kernel, out_shape, scratch_shapes, *arrays, scalars=(), space=pltpu.VMEM):
    vmem = pl.BlockSpec(memory_space=pltpu.VMEM)
    return pl.pallas_call(
        kernel,
        out_shape=out_shape,
        in_specs=[pl.BlockSpec(memory_space=pltpu.SMEM)] * len(scalars)
        + [pl.BlockSpec(memory_space=space)] * len(arrays),
        out_specs=jax.tree.map(lambda _: vmem, out_shape),
        scratch_shapes=scratch_shapes,
        compiler_params=pltpu.CompilerParams(vmem_limit_bytes=48 * 1024 * 1024),
        cost_estimate=pl.CostEstimate(flops=1, bytes_accessed=1, transcendentals=0),
    )(*scalars, *arrays)


def products(weights, inputs, ranges, tiles, blocks):
    turned = [blocks.index(place[::-1]) for place in blocks]
    units, count = weights[0].shape[0], len(blocks)
    _, width, depth = inputs[0].shape
    shape = (count, 2, units // 4, width)
    return called(
        functools.partial(product_kernel, ranges, tiles, turned, len(weights)),
        (jax.ShapeDtypeStruct(shape, jnp.float32), jax.ShapeDtypeStruct(shape, jnp.bfloat16)),
        [
            pltpu.VMEM((units, depth), weights[0].dtype),
            pltpu.VMEM((count, width, depth), weights[0].dtype),
            pltpu.SemaphoreType.DMA((len(weights) + len(inputs),)),
        ],
        *weights,
        *inputs,
        space=pl.ANY,
    )


def norm_kernel(position_ref, *refs):
    sums, (out_ref, act) = refs[:-2], refs[-2:]
    total = 0.0
    count, _, width = act.shape
    done = 0
    for kept_ref, came_ref in zip(sums[::2], sums[1::2]):
        for i in range(kept_ref.shape[0]):
            gate = kept_ref[i, 0] + came_ref[i, 0].astype(jnp.float32)
            up = kept_ref[i, 1] + came_ref[i, 1].astype(jnp.float32)
            value = gate / (1.0 + jnp.exp(-gate)) * up
            act[done] = value
            total += value
            done += 1
    inverse = 1.0 / (count * width)
    mean = jnp.sum(total, axis=1, keepdims=True) * inverse
    squares = 0.0
    for i in range(count):
        deviation = act[i] - mean
        squares += deviation * deviation
    scale = lax.rsqrt(jnp.sum(squares, axis=1, keepdims=True) * inverse + 1e-05)
    for i in range(count):
        place = pl.multiple_of(position_ref[i] * width, width)
        out_ref[:, pl.ds(place, width)] = ((act[i] - mean) * scale).astype(out_ref.dtype)


def normalized(positions, *sums):
    count = positions.shape[0]
    _, _, units, width = sums[0].shape
    return called(
        norm_kernel,
        jax.ShapeDtypeStruct((units, count * width), jnp.bfloat16),
        [pltpu.VMEM((count, units, width), jnp.float32)],
        *sums,
        scalars=(positions,),
    )


def local(first_inputs, second_inputs, first_weights, second_weights):
    a, b, c, x, y, zh = (lax.axis_index(name) for name in ("a", "b", "c", "x", "y", "zh"))
    depth, _, units = first_weights.shape
    piece = first_inputs.shape[0]
    tokens = piece * 32
    half, quarter, eighth = units // 2, units // 4, units // 8
    is_first = b == 0
    sent_inputs = jnp.where(is_first, second_inputs, first_inputs)
    own_inputs = jnp.where(is_first, first_inputs, second_inputs)
    own_zh = jnp.concatenate([own_inputs, swap(sent_inputs, "b")], axis=1)
    other_zh = jnp.concatenate(
        [swap(own_inputs, "zh"), move(sent_inputs, ("zh", "b"), lambda zh, b: (zh + 1, b + 1))], axis=1
    )

    def turned_weights(model):
        parts = model.transpose(1, 2, 0).reshape(2, 2, half, depth).swapaxes(0, 1)
        return jnp.where(c == 0, parts, lax.rev(parts, (0,))).reshape(2 * units, depth)

    sent_weights = turned_weights(jnp.where(is_first, second_weights, first_weights))
    own_weights = turned_weights(jnp.where(is_first, first_weights, second_weights))
    split = depth * 3 // 8
    came_one, came_two = swap(sent_weights[:, :split], "b"), swap(sent_weights[:, split:], "b")

    block = jnp.concatenate(
        [jnp.where(zh == 0, own_zh, other_zh), jnp.where(zh == 0, other_zh, own_zh)], axis=0
    )
    block, came_one = lax.optimization_barrier((jnp.stack(direct(block)), came_one))
    own, one, three, far_low, far_high, came_two = ring(block, 0, came_two)
    weights = own_weights, came_one, came_two

    def core_sum(kept, came):
        return (kept + came.astype(jnp.float32)).reshape(-1, 2, 2, quarter, 2 * piece)

    def depth_parts(sums):
        sent = lax.dynamic_index_in_dim(sums, 1 - a, 2, keepdims=False).astype(jnp.bfloat16)
        kept = lax.dynamic_index_in_dim(sums, a, 2, keepdims=False)
        return [kept[:, :, :eighth], kept[:, :, eighth:]], [sent[:, :, :eighth], sent[:, :, eighth:]]

    chunks = (
        [(i, j) for i in range(2) for j in range(2)],
        [(0, 2), (1, 2), (2, 0), (2, 1), (2, 2)],
        [(i, 3) for i in range(3)] + [(3, j) for j in range(4)],
    )
    kept, sent = products(weights, (own, one), ((0, 2), (0, 2)), ((2, 1), (2, 2)), chunks[0])
    came = swap(sent, "c")
    early = products(weights, (own, one, three), ((2, 1), (2, 1), (0, 3)), ((2, 2), (3, 3)), chunks[1])
    early, came, far_low, far_high = lax.optimization_barrier((early, came, far_low, far_high))
    first, first_came = depth_parts(core_sum(kept, came))
    first_came = [swap(part, "a") for part in first_came]
    came = swap(early[1], "c")
    late = products(
        weights,
        (own, one, three, far_low, far_high),
        ((3, 1),) * 3 + ((0, 2),) * 2,
        ((4, 4), (3, 5)),
        chunks[2],
    )
    late, came, first_came = lax.optimization_barrier((late, came, first_came))
    early, early_came = depth_parts(core_sum(early[0], came))
    early_came = [swap(part, "a") for part in early_came]
    late = core_sum(late[0], swap(late[1], "c"))
    late, early_came = lax.optimization_barrier((late, early_came))
    late, late_came = depth_parts(late)
    late_came = [swap(part, "a") for part in late_came]

    inner, outer = jnp.where(c == 0, x, y), jnp.where(c == 0, y, x)
    positions = []
    for i, j in chunks[0] + chunks[1] + chunks[2]:
        mine, yours = outer ^ MASKS[i], inner ^ MASKS[j]
        positions.append(jnp.where(c == 0, mine * 4 + yours, yours * 4 + mine))
    positions = jnp.stack(positions)
    norm = [normalized(positions, first[h], first_came[h], early[h], early_came[h], late[h], late_came[h]) for h in range(2)]

    two = move(norm[0], ("b",), lambda b: (0,) if b == 1 else None)
    came = [
        move(norm[h], ("x", "a", "b"), lambda x, a, b: (2 * a + h, x // 2, x % 2) if b == 0 else None)
        for h in range(2)
    ]
    one = jnp.where(x % 2 == 0, came[0], came[1])
    two, one = lax.optimization_barrier((jnp.where(is_first, two, norm[1]), one))
    two = lax.all_gather(two, ("zh", "a", "b"), axis=0, tiled=True)
    one = ring(jnp.stack(direct(one)), 2)
    one = jnp.stack([*one[:3], jnp.concatenate(one[3:], axis=2)]).reshape(4 * half, tokens)
    two, one = lax.optimization_barrier((two, one))

    def score(columns):
        result = lax.dot_general(one, columns, (((1,), (1,)), ((), ())), preferred_element_type=jnp.float32)
        return (result * float(tokens) ** (-0.5)).astype(jnp.bfloat16)

    other = swap(two, "c")
    mine, other = lax.optimization_barrier((score(two), other))
    other = score(other)
    low, high = jnp.where(c == 0, mine, other), jnp.where(c == 0, other, mine)
    scores = jnp.concatenate([low[:, :half], high[:, :half], low[:, half:], high[:, half:]], axis=1)
    scores = scores.reshape(4, 4, eighth, 4 * half)
    scores = jnp.where(c == 0, scores, scores.swapaxes(0, 1))
    scores = absolute(scores, x, 1).reshape(4, half, 4 * half)
    came = [scores[0]] + [
        move(scores[i], ("y",), lambda y: (y ^ MASKS[i],)) for i in range(1, 4)
    ]
    came = absolute(jnp.stack(came), y, 0)
    return jnp.concatenate([came[i] for i in range(4)], axis=1).astype(jnp.float32)


def solution(mesh):
    fine = Mesh(mesh.devices.reshape([SIZES[axis] for axis in AXES]), AXES)
    specs = (
        P(("y", "zh", "x"), ("a", "b", "c")),
        P(("y", "zh", "x"), ("a", "b", "c")),
        P(("a", "b", "c"), None, ("y", "zh", "x")),
        P(("a", "b", "c"), None, ("x", "y", "zh")),
    )
    return jax.shard_map(
        local, mesh=fine, in_specs=specs, out_specs=P(("y", "zh", "a", "b", "c"), "x"), check_vma=False
    )
```

```python
import functools
import itertools

import jax
import jax.numpy as jnp
from jax import lax
from jax.experimental import pallas as pl
from jax.experimental.pallas import tpu as pltpu
from jax.sharding import Mesh, PartitionSpec as P

AXES = ("y", "zh", "x", "a", "b", "c")
SIZES = dict(y=4, zh=2, x=4, a=2, b=2, c=2)


def move(value, axes, target):
    sizes = [SIZES[axis] for axis in axes]
    pairs = []
    for source, place in enumerate(itertools.product(*[range(size) for size in sizes])):
        goal = target(**dict(zip(axes, place)))
        if goal is None:
            continue
        index = 0
        for size, coordinate in zip(sizes, goal):
            index = index * size + coordinate % size
        pairs.append((source, index))
    return lax.ppermute(value, axes, pairs)


def swap(value, axis):
    return move(value, (axis,), lambda **place: (place[axis] + 1,))


MASKS = (0, 1, 3, 2)


def plane(value, stage, mask):
    return move(
        value, ("y", "x", "c"), lambda y, x, c: (y, x ^ mask, c) if c == stage else (y ^ mask, x, c)
    )


def direct(value):
    return value, plane(value, 0, 1), plane(value, 0, 3), plane(value, 0, 2)


def ring(value, cut, *first):
    one = plane(value, 1, 1)
    three = plane(value, 1, 3)
    if first:
        one, three, *first = lax.optimization_barrier((one, three, *first))
    half = value.shape[cut] // 2
    far_low = plane(lax.slice_in_dim(one, 0, half, axis=cut), 1, 3)
    far_high = plane(lax.slice_in_dim(three, half, 2 * half, axis=cut), 1, 1)
    return value, one, three, far_low, far_high, *first


def absolute(value, me, dim):
    shape = value.shape
    value = value.reshape(*shape[:dim], 2, 2, *shape[dim + 1 :])
    low, high = (lax.index_in_dim(value, i, dim) for i in range(2))
    value = jnp.concatenate([low, lax.rev(high, (dim + 1,))], axis=dim)
    value = jnp.where(me % 2 == 0, value, lax.rev(value, (dim + 1,)))
    value = jnp.where(me // 2 == 0, value, lax.rev(value, (dim,)))
    return value.reshape(shape)


def product_kernel(ranges, tiles, turned, count, *refs):
    weights, inputs = refs[:count], refs[count : count + len(ranges)]
    kept_ref, sent_ref, held_weights, held, arrived = refs[count + len(ranges) :]
    width = inputs[0].shape[1]
    pieces, column, row = [], 0, 0
    for ref in weights:
        pieces.append((ref, held_weights.at[:, pl.ds(column, ref.shape[1])]))
        column += ref.shape[1]
    for ref, (start, blocks) in zip(inputs, ranges):
        pieces.append((ref.at[pl.ds(start, blocks)], held.at[pl.ds(row, blocks)]))
        row += blocks
    copies = [pltpu.make_async_copy(*piece, arrived.at[i]) for i, piece in enumerate(pieces)]
    for copy in copies:
        copy.start()
    for copy in copies[:count]:
        copy.wait()
    done, waited = 0, count
    for blocks, needed in tiles:
        for copy in copies[waited : count + needed]:
            copy.wait()
        waited = count + needed
        sums = lax.dot_general(
            held_weights[...],
            held[done : done + blocks].reshape(blocks * width, column),
            (((1,), (1,)), ((), ())),
            preferred_element_type=jnp.float32,
        )
        for i in range(blocks):
            block = sums[:, i * width : (i + 1) * width].reshape(2, *kept_ref.shape[1:])
            kept_ref[done + i] = block[0]
            sent_ref[turned[done + i]] = block[1].astype(sent_ref.dtype)
        done += blocks


def called(kernel, out_shape, scratch_shapes, *arrays, scalars=(), space=pltpu.VMEM):
    vmem = pl.BlockSpec(memory_space=pltpu.VMEM)
    return pl.pallas_call(
        kernel,
        out_shape=out_shape,
        in_specs=[pl.BlockSpec(memory_space=pltpu.SMEM)] * len(scalars)
        + [pl.BlockSpec(memory_space=space)] * len(arrays),
        out_specs=jax.tree.map(lambda _: vmem, out_shape),
        scratch_shapes=scratch_shapes,
        compiler_params=pltpu.CompilerParams(vmem_limit_bytes=48 * 1024 * 1024),
        cost_estimate=pl.CostEstimate(flops=1, bytes_accessed=1, transcendentals=0),
    )(*scalars, *arrays)


def products(weights, inputs, ranges, tiles, blocks):
    turned = [blocks.index(place[::-1]) for place in blocks]
    units, count = weights[0].shape[0], len(blocks)
    _, width, depth = inputs[0].shape
    shape = (count, 2, units // 4, width)
    return called(
        functools.partial(product_kernel, ranges, tiles, turned, len(weights)),
        (jax.ShapeDtypeStruct(shape, jnp.float32), jax.ShapeDtypeStruct(shape, jnp.bfloat16)),
        [
            pltpu.VMEM((units, depth), weights[0].dtype),
            pltpu.VMEM((count, width, depth), weights[0].dtype),
            pltpu.SemaphoreType.DMA((len(weights) + len(inputs),)),
        ],
        *weights,
        *inputs,
        space=pl.ANY,
    )


def norm_kernel(position_ref, *refs):
    sums, (out_ref, act) = refs[:-2], refs[-2:]
    total = 0.0
    count, _, width = act.shape
    done = 0
    for kept_ref, came_ref in zip(sums[::2], sums[1::2]):
        for i in range(kept_ref.shape[0]):
            gate = kept_ref[i, 0] + came_ref[i, 0].astype(jnp.float32)
            up = kept_ref[i, 1] + came_ref[i, 1].astype(jnp.float32)
            value = gate / (1.0 + jnp.exp(-gate)) * up
            act[done] = value
            total += value
            done += 1
    inverse = 1.0 / (count * width)
    mean = jnp.sum(total, axis=1, keepdims=True) * inverse
    squares = 0.0
    for i in range(count):
        deviation = act[i] - mean
        squares += deviation * deviation
    scale = lax.rsqrt(jnp.sum(squares, axis=1, keepdims=True) * inverse + 1e-05)
    for i in range(count):
        place = pl.multiple_of(position_ref[i] * width, width)
        out_ref[:, pl.ds(place, width)] = ((act[i] - mean) * scale).astype(out_ref.dtype)


def normalized(positions, *sums):
    count = positions.shape[0]
    _, _, units, width = sums[0].shape
    return called(
        norm_kernel,
        jax.ShapeDtypeStruct((units, count * width), jnp.bfloat16),
        [pltpu.VMEM((count, units, width), jnp.float32)],
        *sums,
        scalars=(positions,),
    )


def local(first_inputs, second_inputs, first_weights, second_weights):
    a, b, c, x, y, zh = (lax.axis_index(name) for name in ("a", "b", "c", "x", "y", "zh"))
    depth, _, units = first_weights.shape
    piece = first_inputs.shape[0]
    tokens = piece * 32
    half, quarter, eighth = units // 2, units // 4, units // 8
    is_first = b == 0
    sent_inputs = jnp.where(is_first, second_inputs, first_inputs)
    own_inputs = jnp.where(is_first, first_inputs, second_inputs)
    own_zh = jnp.concatenate([own_inputs, swap(sent_inputs, "b")], axis=1)
    other_zh = jnp.concatenate(
        [swap(own_inputs, "zh"), move(sent_inputs, ("zh", "b"), lambda zh, b: (zh + 1, b + 1))], axis=1
    )

    def turned_weights(model):
        parts = model.transpose(1, 2, 0).reshape(2, 2, half, depth).swapaxes(0, 1)
        return jnp.where(c == 0, parts, lax.rev(parts, (0,))).reshape(2 * units, depth)

    sent_weights = turned_weights(jnp.where(is_first, second_weights, first_weights))
    own_weights = turned_weights(jnp.where(is_first, first_weights, second_weights))
    split = depth * 3 // 8
    came_one, came_two = swap(sent_weights[:, :split], "b"), swap(sent_weights[:, split:], "b")

    block = jnp.concatenate(
        [jnp.where(zh == 0, own_zh, other_zh), jnp.where(zh == 0, other_zh, own_zh)], axis=0
    )
    block, came_one = lax.optimization_barrier((jnp.stack(direct(block)), came_one))
    own, one, three, far_low, far_high, came_two = ring(block, 0, came_two)
    weights = own_weights, came_one, came_two

    def core_sum(kept, came):
        return (kept + came.astype(jnp.float32)).reshape(-1, 2, 2, quarter, 2 * piece)

    def halves(value):
        return [value[:, :, :eighth], value[:, :, eighth:]]

    def depth_parts(sums):
        sent = lax.dynamic_index_in_dim(sums, 1 - a, 2, keepdims=False).astype(jnp.bfloat16)
        kept = lax.dynamic_index_in_dim(sums, a, 2, keepdims=False)
        return halves(kept), sent

    chunks = (
        [(i, j) for i in range(2) for j in range(2)],
        [(0, 2), (1, 2), (2, 0), (2, 1), (2, 2)],
        [(i, 3) for i in range(3)] + [(3, j) for j in range(4)],
    )
    kept, sent = products(weights, (own, one), ((0, 2), (0, 2)), ((2, 1), (2, 2)), chunks[0])
    came = swap(sent, "c")
    early = products(weights, (own, one, three), ((2, 1), (2, 1), (0, 3)), ((2, 2), (3, 3)), chunks[1])
    early, came, far_low, far_high = lax.optimization_barrier((early, came, far_low, far_high))
    first, first_came = depth_parts(core_sum(kept, came))
    first_came = swap(first_came, "a")
    came = swap(early[1], "c")
    late = products(
        weights,
        (own, one, three, far_low, far_high),
        ((3, 1),) * 3 + ((0, 2),) * 2,
        ((4, 4), (3, 5)),
        chunks[2],
    )
    late, came, first_came = lax.optimization_barrier((late, came, first_came))
    early, early_came = depth_parts(core_sum(early[0], came))
    early_came = swap(early_came, "a")
    late = core_sum(late[0], swap(late[1], "c"))
    late, early_came = lax.optimization_barrier((late, early_came))
    late, late_came = depth_parts(late)
    late_came = [swap(part, "a") for part in halves(late_came)]
    first_came, early_came = halves(first_came), halves(early_came)

    inner, outer = jnp.where(c == 0, x, y), jnp.where(c == 0, y, x)
    positions = []
    for i, j in chunks[0] + chunks[1] + chunks[2]:
        mine, yours = outer ^ MASKS[i], inner ^ MASKS[j]
        positions.append(jnp.where(c == 0, mine * 4 + yours, yours * 4 + mine))
    positions = jnp.stack(positions)
    norm = [normalized(positions, first[h], first_came[h], early[h], early_came[h], late[h], late_came[h]) for h in range(2)]

    two = move(norm[0], ("b",), lambda b: (0,) if b == 1 else None)
    came = [
        move(norm[h], ("x", "a", "b"), lambda x, a, b: (2 * a + h, x // 2, x % 2) if b == 0 else None)
        for h in range(2)
    ]
    one = jnp.where(x % 2 == 0, came[0], came[1])
    two, one = lax.optimization_barrier((jnp.where(is_first, two, norm[1]), one))
    two = lax.all_gather(two, ("zh", "a", "b"), axis=0, tiled=True)
    one = ring(jnp.stack(direct(one)), 2)
    one = jnp.stack([*one[:3], jnp.concatenate(one[3:], axis=2)]).reshape(4 * half, tokens)
    two, one = lax.optimization_barrier((two, one))

    def score(columns):
        result = lax.dot_general(one, columns, (((1,), (1,)), ((), ())), preferred_element_type=jnp.float32)
        return (result * float(tokens) ** (-0.5)).astype(jnp.bfloat16)

    other = swap(two, "c")
    mine, other = lax.optimization_barrier((score(two), other))
    other = score(other)
    low, high = jnp.where(c == 0, mine, other), jnp.where(c == 0, other, mine)
    scores = jnp.concatenate([low[:, :half], high[:, :half], low[:, half:], high[:, half:]], axis=1)
    scores = scores.reshape(4, 4, eighth, 4 * half)
    scores = jnp.where(c == 0, scores, scores.swapaxes(0, 1))
    scores = absolute(absolute(scores, y, 0), x, 1).reshape(4, half, 4 * half)
    scores = lax.all_to_all(scores, "y", 0, 0, tiled=True)
    return jnp.concatenate([scores[i] for i in range(4)], axis=1).astype(jnp.float32)


def solution(mesh):
    fine = Mesh(mesh.devices.reshape([SIZES[axis] for axis in AXES]), AXES)
    specs = (
        P(("y", "zh", "x"), ("a", "b", "c")),
        P(("y", "zh", "x"), ("a", "b", "c")),
        P(("a", "b", "c"), None, ("y", "zh", "x")),
        P(("a", "b", "c"), None, ("x", "y", "zh")),
    )
    return jax.shard_map(
        local, mesh=fine, in_specs=specs, out_specs=P(("y", "zh", "a", "b", "c"), "x"), check_vma=False
    )
```
